512 devices in a mesh: dp: 16 (over y_hi, x), shard: 32 (over y_lo, z, core).
Axes of the slice: x: 4, y: 8 (y_hi: 4, y_lo: 2; y = y_hi * 2 + y_lo), z: 8, core: 2. Of those that a mesh axis runs over, the one named last changes fastest.
Arguments:
- grad_parts: bfloat16 [16, 1024, 512], P('dp', 'shard')
- params: float32 [1024, 512], P('shard'), may hold values from -6 to 6
- momentum: float32 [1024, 512], P('shard'), may hold values from -6 to 6
- statistics: float32 [16384, 512], P('shard')
- stale_roots: bfloat16 [16384, 512], P('shard')
- owners: int32 [4], replicated, may hold values from 0 to 31, as said below
- refresh: int32 [2], replicated, may hold values 0 or 1
Outputs:
- new_params: float32 [1024, 512], P('shard')
- new_momentum: float32 [1024, 512], P('shard')
The draws below stay inside these ranges and needn't reach their ends.
Inputs may be any that keep to these rules, and one draw needn't show every extreme that they name: Distinct slots; factor f's statistic and stale root sit at slot owners[f].
All inputs are finite; a program needn't handle non-finite values. Where the reference program divides by a largest or mean magnitude, that divisor is 1e-20 or more.
Results may differ from the reference program's by a relative error of at most 0.0095.
Values may be sent and summed in bfloat16 or wider, within the bound.
A program may use at most 64 MiB of HBM per device.

```python
import jax
import jax.numpy as jnp
from jax import lax

B = 512
ROWS = 32
ITERS = 4
NBLK = 2
NFAC = 4
N_DP = 16
N_SHARD = 32


def draw_grad_parts(key, part):
    key = jax.random.fold_in(key, 14)
    keys = jax.random.split(key, 7)
    rows_all = NBLK * B
    position = (jnp.arange(B, dtype=jnp.float32) + 0.5) * (2.0 / B) - 1.0
    signs = jax.random.rademacher(keys[0], (NBLK, 1), dtype=jnp.float32)
    slopes = jax.random.uniform(keys[1], (NBLK, 1), jnp.float32, 0.55, 0.8)
    ramp = (signs * slopes * position[None, :]).reshape(rows_all)
    levels = jax.random.uniform(keys[2], (rows_all // ROWS, 1), jnp.float32, -0.5, 0.5)
    levels = jnp.broadcast_to(levels, (rows_all // ROWS, ROWS)).reshape(rows_all)
    jitter = jax.random.uniform(keys[3], (rows_all,), jnp.float32, -0.3, 0.3)
    row_scale = jnp.exp(ramp + levels + jitter)
    col_scale = jnp.exp(jax.random.uniform(keys[4], (B,), jnp.float32, -0.6, 0.6))
    common = jnp.clip(jax.random.normal(keys[5], (NBLK, 1, B), jnp.float32), -4.0, 4.0)
    common = jnp.broadcast_to(common, (NBLK, B, B)).reshape(rows_all, B)
    noise = jnp.clip(jax.random.normal(keys[6], (N_DP, rows_all, B), jnp.float32), -4.0, 4.0)
    weight = 1.2
    shared = weight * N_DP ** (-0.5) * common
    values = row_scale[None, :, None] * col_scale[None, None, :] * (shared[None] + noise)
    return values.astype(jnp.bfloat16)


def draw_statistics(key, part):
    key = jax.random.fold_in(key, 11)
    first = jax.random.fold_in(key, 0)
    offset = (12.0 / B) ** 0.5
    factors = jax.random.normal(first, (N_SHARD, B, 2 * B), jnp.float32) + offset
    gram = jnp.einsum('nij,nkj->nik', factors, factors, precision=lax.Precision.HIGHEST)
    gram = gram + 0.1 * (2 * B) * jnp.eye(B, dtype=jnp.float32)[None]
    return gram.reshape(N_SHARD * B, B)


def draw_stale_roots(key, part):
    key = jax.random.fold_in(key, 12)
    first, second = jax.random.split(key)
    level = (2.0 * B) ** (-0.25)
    diag = level * jnp.exp(jax.random.uniform(first, (N_SHARD, B), jnp.float32, -0.7, 0.7))
    noise = jax.random.uniform(second, (N_SHARD, B, B), jnp.float32, -1.0, 1.0)
    offdiag = 0.5 * level * (noise + jnp.swapaxes(noise, 1, 2)) * B ** (-0.5)
    eye = jnp.eye(B, dtype=jnp.float32)[None]
    damping = 0.7 * level / B * jnp.ones((1, B, B), jnp.float32)
    return (diag[:, :, None] * eye + offdiag - damping).reshape(N_SHARD * B, B).astype(jnp.bfloat16)


def draw_owners(key, part):
    key = jax.random.fold_in(key, 13)
    first, second = jax.random.split(key)
    middle = 1 + jax.random.permutation(first, N_SHARD - 2)[:NFAC - 2].astype(jnp.int32)
    ends = jnp.array([0, N_SHARD - 1], dtype=jnp.int32)
    chosen = jnp.concatenate([ends, middle])
    order = jax.random.permutation(second, NFAC)
    return chosen[order].astype(jnp.int32)


def touch_ends(drawn, stream_key, low, top_value):
    longest = drawn.shape.index(max(drawn.shape))
    spots = []
    for shift in (0, 1):
        where = [jax.random.randint(jax.random.fold_in(stream_key, axis), (), 0, length) for axis, length in enumerate(drawn.shape)]
        where[longest] = (where[longest] + shift) % drawn.shape[longest]
        spots.append(tuple(where))
    return drawn.at[spots[0]].set(low).at[spots[1]].set(top_value)


def steps_of(stream_key, shape, shards, least, largest):
    factor_of = 1.0
    for axis_at, shards_of in shards:
        heights = jax.random.uniform(jax.random.fold_in(jax.random.fold_in(stream_key, 6), axis_at), (shards_of,), jnp.float32, least / len(shards), largest / len(shards))
        factor_of = factor_of * jnp.repeat(jnp.exp(heights), shape[axis_at] // shards_of).reshape((-1,) + (1,) * (len(shape) - 1 - axis_at))
    return factor_of


def gaussian(key, extent, scale, most, pieces=(), kind=jnp.bfloat16):
    factor_of = steps_of(key, extent, pieces, -0.22, 0.18) if pieces else 1.0
    values = jax.random.normal(key, extent, jnp.float32) * scale * factor_of
    return jnp.minimum(jnp.maximum(values, -most), most).astype(kind)


def setup_inputs(seed: int = 0) -> dict:
    streams_of = jax.random.split(jax.random.key(seed), 8)
    grad_parts = draw_grad_parts(jax.random.fold_in(streams_of[7], 71), 0)
    params = gaussian(streams_of[1], (NBLK * B, B), 1.0, 6.0, ((0, 32),), jnp.float32)
    momentum = gaussian(streams_of[2], (NBLK * B, B), 1.0, 6.0, ((0, 32),), jnp.float32)
    statistics = draw_statistics(jax.random.fold_in(streams_of[7], 71), 0)
    stale_roots = draw_stale_roots(jax.random.fold_in(streams_of[7], 71), 0)
    owners = draw_owners(jax.random.fold_in(streams_of[7], 71), 0)
    refresh = touch_ends((jax.random.randint(streams_of[6], (NBLK,), 0, 2) < 1).astype(jnp.int32), jax.random.fold_in(streams_of[6], 1), 0, 1)
    return dict(grad_parts=grad_parts, params=params, momentum=momentum, statistics=statistics, stale_roots=stale_roots, owners=owners, refresh=refresh)


def inverse_root(stat):
    size = stat.shape[0]
    eye = jnp.eye(size, dtype=jnp.float32)
    bound = jnp.max(lax.optimization_barrier(jnp.sum(jnp.abs(stat), axis=1)))
    matrix = stat / bound
    factor = (5.0 * eye - matrix) * 0.25
    result = factor * bound ** (-0.25)
    for step in range(1, ITERS):
        square = jnp.dot(factor, factor, precision=lax.Precision.HIGHEST)
        fourth = jnp.dot(square, square, precision=lax.Precision.HIGHEST)
        matrix = jnp.dot(fourth, matrix, precision=lax.Precision.HIGHEST)
        factor = (5.0 * eye - matrix) * 0.25
        result = jnp.dot(result, factor, precision=lax.Precision.HIGHEST)
    return result

def reference(grad_parts, params, momentum, statistics, stale_roots, owners, refresh):
    summed = lax.optimization_barrier(jnp.sum(grad_parts.astype(jnp.float32), axis=0))
    grad = (summed / N_DP).astype(jnp.bfloat16)
    stat_slots = statistics.reshape(N_SHARD, B, B)
    root_slots = stale_roots.reshape(N_SHARD, B, B)

    def one_factor(index):
        slot = owners[index]
        fresh = inverse_root(stat_slots[slot]).astype(jnp.bfloat16)
        return jnp.where(refresh[index // 2] > 0, fresh, root_slots[slot])
    roots = lax.map(one_factor, jnp.arange(NFAC, dtype=jnp.int32))
    blocks = grad.reshape(NBLK, B, B).astype(jnp.float32)
    lefts = roots[0::2].astype(jnp.float32)
    rights = roots[1::2].astype(jnp.float32)
    image = jnp.einsum('kij,kjl->kil', blocks, rights).astype(jnp.bfloat16)
    precond = jnp.einsum('kij,kjl->kil', lefts, image.astype(jnp.float32))
    grad_sq = lax.optimization_barrier(jnp.sum(blocks * blocks, axis=(1, 2)))
    prec_sq = lax.optimization_barrier(jnp.sum(precond * precond, axis=(1, 2)))
    scale = jnp.sqrt(grad_sq) * lax.rsqrt(prec_sq + 1e-06)
    direction = (precond * scale[:, None, None]).reshape(NBLK * B, B)
    new_momentum = 0.9 * momentum + direction
    new_params = params - 0.1 * new_momentum
    return (new_params, new_momentum)
```

```python
import functools

import jax
import jax.numpy as jnp
from jax import lax
from jax.experimental import pallas as pl
from jax.experimental.pallas import tpu as pltpu
from jax.sharding import PartitionSpec as P

MESH = pl.DeviceIdType.MESH
F32 = jnp.float32
BF16 = jnp.bfloat16
NT = (((1,), (1,)), ((), ()))
NN = (((1,), (0,)), ((), ()))
SMALL = 2.0 ** -20


def dot(a, b, dims=NN):
    return lax.dot_general(a, b, dims, preferred_element_type=F32)


def halves(value):
    high = value.astype(BF16)
    return high, (value - high.astype(F32)).astype(BF16)


def swap4(tiles, quarter):
    out = []
    for q in range(4):
        total = tiles[0] if q == 0 else pltpu.roll(tiles[0], (-32 * q) % 128, 1)
        for p in range(1, 4):
            part = tiles[p] if p == q else pltpu.roll(tiles[p], (32 * (p - q)) % 128, 1)
            total = jnp.where(quarter == p, part, total)
        out.append(total)
    return out


def kernel(
    nd, ns, owners, refresh, grad_hbm, stat_hbm, stale_hbm, out_ref,
    grad_v, stat_v, stale_v, mh, ml, rs_buf, gp, x_send, x_buf, l_send, r_send,
    l_buf, r_buf, lt_v, t_send, t_buf, n_buf, local_sem, send_sem, recv_sem,
):
    width = stat_v.shape[0]
    nh = ns // 2
    groups = width // 128
    pieces = 2 * groups
    d = lax.axis_index("dp")
    s = lax.axis_index("shard")
    block = s // nh
    t = s % nh
    mine = d % pieces
    span = 16 * nh

    barrier = pltpu.get_barrier_semaphore()

    @pl.loop(1, ns)
    def _(k):
        pl.semaphore_signal(
            barrier, inc=1, device_id=(d, lax.rem(s + k, ns)), device_id_type=MESH
        )

    @pl.loop(1, nd)
    def _(k):
        pl.semaphore_signal(
            barrier, inc=1, device_id=(lax.rem(d + k, nd), s), device_id_type=MESH
        )

    load_grad = pltpu.make_async_copy(grad_hbm.at[0], grad_v, local_sem.at[0])
    load_stat = pltpu.make_async_copy(stat_hbm, stat_v, local_sem.at[1])
    load_stale = pltpu.make_async_copy(stale_hbm, stale_v, local_sem.at[2])
    load_grad.start()
    load_stat.start()
    load_stale.start()

    def send(phase, src, dst, dp, shard):
        pltpu.make_async_remote_copy(
            src_ref=src, dst_ref=dst, send_sem=send_sem.at[phase],
            recv_sem=recv_sem.at[phase], device_id=(dp, shard), device_id_type=MESH,
        ).start()

    def whole(phase, ref):
        return pltpu.make_async_remote_copy(
            src_ref=ref, dst_ref=ref, send_sem=send_sem.at[phase],
            recv_sem=recv_sem.at[phase], device_id=(lax.rem(d + 1, nd), s), device_id_type=MESH,
        )

    def grad_piece(which):
        row = pl.multiple_of(which // groups * 16, 16)
        column = pl.multiple_of(which % groups * 128, 128)
        return grad_v.at[pl.ds(row, 16), pl.ds(column, 128)]

    load_grad.wait()
    rs_buf[d] = grad_piece(mine)[...]
    pl.semaphore_wait(barrier, ns + nd - 2)

    @pl.loop(1, nd)
    def _(k):
        other = lax.rem(d + k, nd)
        send(0, grad_piece(other % pieces), rs_buf.at[d], other, s)

    load_stat.wait()
    tall = 128
    blocks = width // tall

    def row_sums(r, most):
        rows = pl.ds(pl.multiple_of(r * tall, tall), tall)
        return jnp.maximum(most, jnp.sum(jnp.abs(stat_v[rows]), axis=1, keepdims=True))

    most = lax.fori_loop(0, blocks, row_sums, jnp.zeros((tall, 1), F32))
    bound = jnp.max(most, axis=0, keepdims=True)
    inverse = 1.0 / (bound * SMALL)

    @pl.loop(0, blocks)
    def _(r):
        rows = pl.ds(pl.multiple_of(r * tall, tall), tall)
        mh[0, rows], ml[0, rows] = halves((stat_v[rows] * SMALL) * inverse)

    def product(first, second, result, alpha, beta):
        high = min(width, 256)

        @pl.loop(0, width // high)
        def _(r):
            rows = pl.ds(pl.multiple_of(r * high, high), high)
            ah, al = mh[first, rows], ml[first, rows]
            total = dot(ah, mh[second]) + (dot(ah, ml[second]) + dot(al, mh[second]))
            kept = mh[second, rows].astype(F32) + ml[second, rows].astype(F32)
            mh[result, rows], ml[result, rows] = halves(alpha * kept + beta * total)

    def newton(base):
        @pl.loop(0, 3)
        def _(k):
            alpha = jnp.where(k == 0, -0.625, jnp.where(k == 1, 3.125, 2.44140625))
            beta = jnp.where(k == 0, 0.0625, 1.0)
            product(base + k, base + k % 2, base + k + 1, alpha, beta)

    newton(0)

    whole(0, rs_buf.at[pl.ds(0, nd - 1)]).wait_recv()

    def add_part(k, total):
        return total + rs_buf[k].astype(F32)

    summed = lax.fori_loop(1, nd, add_part, rs_buf[0].astype(F32))
    here = pl.ds(pl.multiple_of(t * 16, 16), 16)
    gp[mine, here] = (summed * (1.0 / nd)).astype(BF16)

    @pl.loop(1, nh)
    def _(k):
        spot = gp.at[mine, here]
        send(1, spot, spot, d, block * nh + lax.rem(t + k, nh))

    newton(3)

    whole(1, gp.at[0, pl.ds(0, span - 16)]).wait_recv()

    @pl.loop(1, pieces)
    def _(k):
        spot = gp.at[mine]
        send(2, spot, spot, d // pieces * pieces + lax.rem(mine + k, pieces), s)

    column = lax.broadcasted_iota(jnp.int32, (32, width), 1)
    line = lax.broadcasted_iota(jnp.int32, (32, width), 0)
    picked = jnp.where(column == line + 32 * d, 1.0, 0.0)

    def apply(slot, value, alpha, beta):
        high, low = halves(value)
        total = dot(high, mh[slot], NT) + (dot(high, ml[slot], NT) + dot(low, mh[slot], NT))
        return alpha * value + beta * total

    left = lax.fori_loop(0, 3, lambda k, v: apply(3 * k, v, 1.25, -0.25), picked)

    def right_step(k, v):
        return apply(6, v, jnp.where(k == 0, 0.0, 1.25), jnp.where(k == 0, 1.0, -0.25))

    right = lax.fori_loop(0, 5, right_step, left)
    fresh = (1.25 * left - 0.25 * right) * lax.rsqrt(jnp.sqrt(bound))
    load_stale.wait()
    stale = dot(picked.astype(BF16), stale_v[...], NT)
    flag = jnp.int32(0)
    for f in range(4):
        flag = flag + jnp.where(owners[f] == s, refresh[f // 2], 0)
    chosen = jnp.full((32, width), flag, jnp.int32) > 0
    root = jnp.where(chosen, fresh.astype(BF16).astype(F32), stale)

    quarter = lax.broadcasted_iota(jnp.int32, (8, 128), 1) // 32
    for g in range(groups):
        tiles = swap4([root[8 * q:8 * q + 8, 128 * g:128 * g + 128] for q in range(4)], quarter)
        for p in range(4):
            x_send[4 * g + p] = tiles[p]
    x_buf[s] = x_send[t]

    @pl.loop(1, ns)
    def _(k):
        other = lax.rem(s + k, ns)
        send(3, x_send.at[lax.rem(other, nh)], x_buf.at[s], d, other)

    whole(3, x_buf.at[pl.ds(0, ns - 1)]).wait_recv()

    piece = x_buf[owners[2 * block + 1]]
    r_send[...] = piece
    r_buf[t] = piece
    piece = x_buf[owners[2 * block]]
    l_send[...] = piece
    l_buf[d] = piece

    @pl.loop(1, nh)
    def _(k):
        send(4, r_send, r_buf.at[t], d, block * nh + lax.rem(t + k, nh))

    @pl.loop(1, nd)
    def _(k):
        send(5, l_send, l_buf.at[d], lax.rem(d + k, nd), s)

    whole(2, gp.at[pl.ds(0, pieces - 1)]).wait_recv()

    def grad_square(k, total):
        tile = gp[k].astype(F32)
        tile = tile * tile
        return total + jnp.sum(tile.reshape(span // 8, 8, 128), axis=0)

    grad_sq = lax.fori_loop(0, pieces, grad_square, jnp.zeros((8, 128), F32))

    whole(4, r_buf.at[pl.ds(0, nh - 1)]).wait_recv()
    parts = [swap4([r_buf[4 * g + p] for p in range(4)], quarter) for g in range(groups)]
    rights = [jnp.concatenate(part, 0).astype(BF16) for part in parts]
    image = []
    for h in range(2):
        total = dot(rights[0], gp[h * groups], NT)
        for g in range(1, groups):
            total = total + dot(rights[g], gp[h * groups + g], NT)
        image.append(total.astype(BF16))
    image = jnp.concatenate(image, 1)

    whole(5, l_buf.at[pl.ds(0, nd - 1)]).wait_recv()
    for k in range(nd):
        tile = l_buf[k]
        for q in range(4):
            row = q // 2 * span + 16 * k + q % 2 * 8
            lt_v[row:row + 8] = tile if q == 0 else pltpu.roll(tile, (-32 * q) % 128, 1)
    turned = dot(image, lt_v[...].astype(BF16))
    turned = jnp.concatenate([turned, jnp.zeros((96, 128), F32)], 0).T
    tile = turned[0:8]
    for q in range(1, 4):
        tile = jnp.where(quarter == q, pltpu.roll(turned[8 * q:8 * q + 8], 32 * q, 1), tile)
    t_send[...] = tile
    t_buf[d] = tile

    @pl.loop(1, nd)
    def _(k):
        send(6, t_send, t_buf.at[d], lax.rem(d + k, nd), s)

    whole(6, t_buf.at[pl.ds(0, nd - 1)]).wait_recv()
    rows = [swap4([t_buf[4 * g + p] for p in range(4)], quarter) for g in range(groups)]
    square = sum(tile * tile for part in rows for tile in part)
    n_buf[t] = square

    @pl.loop(1, nh)
    def _(k):
        spot = n_buf.at[t]
        send(7, spot, spot, d, block * nh + lax.rem(t + k, nh))

    grad_sum = jnp.sum(jnp.sum(grad_sq, axis=1, keepdims=True), axis=0, keepdims=True)
    whole(7, n_buf.at[pl.ds(0, nh - 1)]).wait_recv()
    square = sum(n_buf[k] for k in range(nh))
    square = jnp.sum(jnp.sum(square, axis=1, keepdims=True), axis=0, keepdims=True)
    scale = jnp.sqrt(grad_sum) * lax.rsqrt(square + 1e-6)
    for g in range(groups):
        for q in range(4):
            out_ref[8 * q:8 * q + 8, 128 * g:128 * g + 128] = rows[g][q] * scale

    whole(0, rs_buf.at[pl.ds(0, nd - 1)]).wait_send()
    whole(1, gp.at[0, pl.ds(0, span - 16)]).wait_send()
    whole(2, gp.at[pl.ds(0, pieces - 1)]).wait_send()
    whole(3, x_buf.at[pl.ds(0, ns - 1)]).wait_send()
    whole(4, r_buf.at[pl.ds(0, nh - 1)]).wait_send()
    whole(5, l_buf.at[pl.ds(0, nd - 1)]).wait_send()
    whole(6, t_buf.at[pl.ds(0, nd - 1)]).wait_send()
    whole(7, n_buf.at[pl.ds(0, nh - 1)]).wait_send()


def per_device(nd, ns, grad_parts, params, momentum, statistics, stale_roots, owners, refresh):
    width = params.shape[1]
    nh = ns // 2
    groups = width // 128
    hbm = pl.BlockSpec(memory_space=pl.ANY)
    smem = pl.BlockSpec(memory_space=pltpu.SMEM)
    tile = pltpu.VMEM((8, 128), F32)
    direction = pl.pallas_call(
        functools.partial(kernel, nd, ns),
        out_shape=jax.ShapeDtypeStruct(params.shape, F32),
        in_specs=[smem, smem, hbm, hbm, hbm],
        out_specs=pl.BlockSpec(memory_space=pltpu.VMEM),
        scratch_shapes=[
            pltpu.VMEM(params.shape, BF16),
            pltpu.VMEM((width, width), F32),
            pltpu.VMEM((width, width), BF16),
            pltpu.VMEM((7, width, width), BF16),
            pltpu.VMEM((7, width, width), BF16),
            pltpu.VMEM((nd, 16, 128), BF16),
            pltpu.VMEM((2 * groups, 16 * nh, 128), BF16),
            pltpu.VMEM((nh, 8, 128), F32),
            pltpu.VMEM((ns, 8, 128), F32),
            tile,
            tile,
            pltpu.VMEM((nd, 8, 128), F32),
            pltpu.VMEM((nh, 8, 128), F32),
            pltpu.VMEM((width, 128), F32),
            tile,
            pltpu.VMEM((nd, 8, 128), F32),
            pltpu.VMEM((nh, 8, 128), F32),
            pltpu.SemaphoreType.DMA((3,)),
            pltpu.SemaphoreType.DMA((8,)),
            pltpu.SemaphoreType.DMA((8,)),
        ],
        compiler_params=pltpu.CompilerParams(
            collective_id=0, has_side_effects=True, vmem_limit_bytes=48 * 2 ** 20
        ),
    )(owners, refresh, grad_parts, statistics, stale_roots)
    new_momentum = 0.9 * momentum + direction
    return params - 0.1 * new_momentum, new_momentum


def solution(mesh):
    rows = P("shard", None)
    body = functools.partial(per_device, mesh.shape["dp"], mesh.shape["shard"])
    return jax.shard_map(
        body,
        mesh=mesh,
        in_specs=(P("dp", "shard", None), rows, rows, rows, rows, P(), P()),
        out_specs=(rows, rows),
        check_vma=False,
    )
```

```python
import functools

import jax
import jax.numpy as jnp
from jax import lax
from jax.experimental import pallas as pl
from jax.experimental.pallas import tpu as pltpu
from jax.sharding import PartitionSpec as P

MESH = pl.DeviceIdType.MESH
F32 = jnp.float32
BF16 = jnp.bfloat16
NT = (((1,), (1,)), ((), ()))
NN = (((1,), (0,)), ((), ()))
SMALL = 2.0 ** -20


def dot(a, b, dims=NN):
    return lax.dot_general(a, b, dims, preferred_element_type=F32)


def halves(value):
    high = value.astype(BF16)
    return high, (value - high.astype(F32)).astype(BF16)


def swap(tiles, part, count):
    size = 128 // count
    out = []
    for q in range(count):
        total = tiles[0] if q == 0 else pltpu.roll(tiles[0], 128 - size * q, 1)
        for p in range(1, count):
            other = tiles[p] if p == q else pltpu.roll(tiles[p], size * (p - q) % 128, 1)
            total = jnp.where(part == p, other, total)
        out.append(total)
    return out


def kernel(
    nd, ns, owners_hbm, refresh_hbm, grad_hbm, stat_hbm, stale_hbm, out_ref,
    owners, refresh, grad_v, stat_v, stale_v, mh, ml, rs_buf, gp, x_send, x_buf, l_send,
    r_send, l_buf, r_buf, lt_v, t_buf, n_buf, local_sem, send_sem, recv_sem,
):
    width = stat_v.shape[0]
    nh = ns // 2
    nz = nh // 2
    groups = width // 128
    pieces = 2 * groups
    nx = groups
    ny = nd // nx
    span = 16 * nz
    d = lax.axis_index("dp")
    s = lax.axis_index("shard")
    x = d % nx
    y = d // nx
    block = s // nh
    t = s % nh
    core = s % 2
    z = t // 2
    mine = d % pieces

    barrier = pltpu.get_barrier_semaphore()

    @pl.loop(1, nd)
    def _(k):
        pl.semaphore_signal(
            barrier, inc=1, device_id=(lax.rem(d + k, nd), s), device_id_type=MESH
        )

    @pl.loop(1, ns)
    def _(k):
        pl.semaphore_signal(
            barrier, inc=1, device_id=(d, lax.rem(s + k, ns)), device_id_type=MESH
        )

    load_grad = pltpu.make_async_copy(grad_hbm.at[0], grad_v, local_sem.at[0])
    load_stat = pltpu.make_async_copy(stat_hbm, stat_v, local_sem.at[1])
    load_stale = pltpu.make_async_copy(stale_hbm, stale_v, local_sem.at[2])
    load_owners = pltpu.make_async_copy(owners_hbm, owners, local_sem.at[3])
    load_refresh = pltpu.make_async_copy(refresh_hbm, refresh, local_sem.at[4])
    load_grad.start()
    load_stat.start()
    load_stale.start()
    load_owners.start()
    load_refresh.start()

    def send(phase, src, dst, dp, shard):
        pltpu.make_async_remote_copy(
            src_ref=src, dst_ref=dst, send_sem=send_sem.at[phase],
            recv_sem=recv_sem.at[phase], device_id=(dp, shard), device_id_type=MESH,
        ).start()

    def whole(phase, ref):
        return pltpu.make_async_remote_copy(
            src_ref=ref, dst_ref=ref, send_sem=send_sem.at[phase],
            recv_sem=recv_sem.at[phase], device_id=(lax.rem(d + 1, nd), s), device_id_type=MESH,
        )

    def send_near(phase, src, dst):
        for k in range(1, nx):
            send(phase, src, dst, y * nx + lax.rem(x + k, nx), s)
        for k in range(nx):
            row = lax.rem(y + (ny - 1 if k % 2 == 0 else 1), ny)
            send(phase, src, dst, row * nx + lax.rem(x + k, nx), s)

    def grad_piece(which):
        row = pl.multiple_of(which // groups * 16, 16)
        column = pl.multiple_of(which % groups * 128, 128)
        return grad_v.at[pl.ds(row, 16), pl.ds(column, 128)]

    load_grad.wait()
    rs_buf[d] = grad_piece(mine)[...]
    pl.semaphore_wait(barrier, ns + nd - 2)

    @pl.loop(1, nd)
    def _(k):
        other = lax.rem(d + k, nd)
        send(0, grad_piece(other % pieces), rs_buf.at[d], other, s)

    load_stat.wait()
    tall = 128
    blocks = width // tall

    def row_sums(r, most):
        rows = pl.ds(pl.multiple_of(r * tall, tall), tall)
        return jnp.maximum(most, jnp.sum(jnp.abs(stat_v[rows]), axis=1, keepdims=True))

    most = lax.fori_loop(0, blocks, row_sums, jnp.zeros((tall, 1), F32))
    bound = jnp.max(most, axis=0, keepdims=True)
    inverse = 1.0 / (bound * SMALL)

    @pl.loop(0, blocks)
    def _(r):
        rows = pl.ds(pl.multiple_of(r * tall, tall), tall)
        mh[0, rows], ml[0, rows] = halves((stat_v[rows] * SMALL) * inverse)

    def product(first, second, result, alpha, beta, both):
        high = min(width, 256)

        @pl.loop(0, width // high)
        def _(r):
            rows = pl.ds(pl.multiple_of(r * high, high), high)
            total = dot(mh[first, rows], mh[second])
            if both:
                total = total + dot(ml[first, rows], mh[second])
            kept = mh[second, rows].astype(F32) + ml[second, rows].astype(F32)
            mh[result, rows], ml[result, rows] = halves(alpha * kept + beta * total)

    @pl.loop(0, 2)
    def _(k):
        base = 3 * k

        @pl.loop(0, 2)
        def _(j):
            alpha = jnp.where(j == 0, -0.625, 3.125)
            beta = jnp.where(j == 0, 0.0625, 1.0)
            product(base + j, base + j, base + j + 1, alpha, beta, False)

        product(base + 2, base, base + 3, 2.44140625, 1.0, True)

    column = lax.broadcasted_iota(jnp.int32, (64, width), 1)
    line = lax.broadcasted_iota(jnp.int32, (64, width), 0)
    picked = jnp.where(column == line + 64 * mine, 1.0, 0.0)

    def apply(slot, value, alpha, beta):
        total = dot(jnp.concatenate(halves(value), 0), mh[slot], NT)
        return alpha * value + beta * (total[:64] + total[64:])

    left = lax.fori_loop(0, 3, lambda k, v: apply(3 * k, v, 1.25, -0.25), picked)

    def right_step(k, v):
        return apply(6, v, jnp.where(k == 0, 0.0, 1.25), jnp.where(k == 0, 1.0, -0.25))

    right = lax.fori_loop(0, 5, right_step, left)
    fresh = (1.25 * left - 0.25 * right) * lax.rsqrt(jnp.sqrt(bound))
    load_stale.wait()
    load_owners.wait()
    load_refresh.wait()
    stale = dot(picked.astype(BF16), stale_v[...], NT)
    flag = jnp.int32(0)
    for f in range(4):
        flag = flag + jnp.where(owners[f] == s, refresh[f // 2], 0)
    chosen = jnp.full((64, width), flag, jnp.int32) > 0
    root = jnp.where(chosen, fresh, stale)

    quarter = lax.broadcasted_iota(jnp.int32, (16, 128), 1) // 32
    half = quarter // 2
    for g in range(groups):
        tiles = [root[16 * q:16 * q + 16, 128 * g:128 * g + 128] for q in range(4)]
        tiles = swap(tiles, quarter, 4)
        for p in range(4):
            x_send[4 * g + p] = tiles[p].astype(BF16)
    x_buf[s] = x_send[t]

    @pl.loop(1, ns)
    def _(k):
        other = lax.rem(s + k, ns)
        send(3, x_send.at[lax.rem(other, nh)], x_buf.at[s], d, other)

    whole(0, rs_buf.at[pl.ds(0, nd - 1)]).wait_recv()
    summed = rs_buf[0].astype(F32)
    for k in range(1, nd):
        summed = summed + rs_buf[k].astype(F32)
    here = pl.ds(pl.multiple_of(z * 16, 16), 16)
    gp[core, mine, here] = (summed * (1.0 / nd)).astype(BF16)

    @pl.loop(1, nz)
    def _(k):
        spot = gp.at[core, mine, here]
        send(1, spot, spot, d, block * nh + lax.rem(t + 2 * k, nh))

    whole(1, gp.at[0, 0, pl.ds(0, span - 16)]).wait_recv()
    send_near(2, gp.at[core, mine], gp.at[core, mine])

    whole(3, x_buf.at[pl.ds(0, ns - 1)]).wait_recv()

    piece = x_buf[owners[2 * block + 1]]
    r_send[...] = piece
    r_buf[t] = piece

    @pl.loop(1, nh)
    def _(k):
        send(4, r_send, r_buf.at[t], d, block * nh + lax.rem(t + k, nh))

    piece = x_buf[owners[2 * block]]
    l_send[...] = piece
    l_buf[mine] = piece
    send_near(5, l_send, l_buf.at[mine])

    whole(5, l_buf.at[pl.ds(0, pieces - 1)]).wait_recv()
    for k in range(pieces):
        tile = l_buf[k].astype(F32)
        for q in range(4):
            row = q * span + 16 * k
            turned = tile if q == 0 else pltpu.roll(tile, 128 - 32 * q, 1)
            lt_v[row:row + 16] = turned.astype(BF16)

    whole(4, r_buf.at[pl.ds(0, nh - 1)]).wait_recv()
    parts = []
    for g in range(groups):
        tiles = [r_buf[4 * g + p].astype(F32) for p in range(4)]
        parts.append(jnp.concatenate(swap(tiles, quarter, 4), 0))
    right_root = jnp.concatenate(parts, 1).astype(BF16)

    whole(2, gp.at[0, pl.ds(0, pieces - 1)]).wait_recv()
    send(8, gp.at[core], gp.at[core], d, s + 1 - 2 * core)
    whole(8, gp.at[0]).wait_recv()
    grad = jnp.concatenate([
        jnp.concatenate([gp[c, h * groups + g] for g in range(groups)], 1)
        for c in range(2) for h in range(2)
    ], 0)
    image = dot(right_root, grad, NT).astype(BF16)
    turned = dot(image, lt_v[...])
    turned = jnp.concatenate([turned, jnp.zeros((64, 128), F32)], 0).T
    tile = jnp.where(half == 0, turned[0:16], pltpu.roll(turned[16:32], 64, 1))
    t_buf[mine] = tile
    send_near(6, t_buf.at[mine], t_buf.at[mine])

    def grad_square(k, total):
        tile = gp[k // pieces, k % pieces].astype(F32)
        tile = tile * tile
        return total + jnp.sum(tile.reshape(span // 8, 8, 128), axis=0)

    grad_sq = lax.fori_loop(0, 2 * pieces, grad_square, jnp.zeros((8, 128), F32))
    grad_sum = jnp.sum(jnp.sum(grad_sq, axis=1, keepdims=True), axis=0, keepdims=True)

    whole(6, t_buf.at[pl.ds(0, pieces - 1)]).wait_recv()
    rows = [swap([t_buf[2 * g], t_buf[2 * g + 1]], half, 2) for g in range(groups)]
    square = sum(tile * tile for part in rows for tile in part)
    n_buf[t] = square[:8] + square[8:]

    @pl.loop(1, nh)
    def _(k):
        spot = n_buf.at[t]
        send(7, spot, spot, d, block * nh + lax.rem(t + k, nh))

    whole(7, n_buf.at[pl.ds(0, nh - 1)]).wait_recv()
    square = sum(n_buf[k] for k in range(nh))
    square = jnp.sum(jnp.sum(square, axis=1, keepdims=True), axis=0, keepdims=True)
    scale = jnp.sqrt(grad_sum) * lax.rsqrt(square + 1e-6)
    for g in range(groups):
        for u in range(2):
            out_ref[16 * u:16 * u + 16, 128 * g:128 * g + 128] = rows[g][u] * scale

    whole(0, rs_buf.at[pl.ds(0, nd - 1)]).wait_send()
    whole(1, gp.at[0, 0, pl.ds(0, span - 16)]).wait_send()
    whole(2, gp.at[0, pl.ds(0, pieces - 1)]).wait_send()
    whole(3, x_buf.at[pl.ds(0, ns - 1)]).wait_send()
    whole(4, r_buf.at[pl.ds(0, nh - 1)]).wait_send()
    whole(5, l_buf.at[pl.ds(0, pieces - 1)]).wait_send()
    whole(6, t_buf.at[pl.ds(0, pieces - 1)]).wait_send()
    whole(7, n_buf.at[pl.ds(0, nh - 1)]).wait_send()
    whole(8, gp.at[0]).wait_send()


def per_device(nd, ns, grad_parts, params, momentum, statistics, stale_roots, owners, refresh):
    width = params.shape[1]
    nh = ns // 2
    pieces = width // 64
    direction = pl.pallas_call(
        functools.partial(kernel, nd, ns),
        out_shape=jax.ShapeDtypeStruct(params.shape, F32),
        in_specs=[pl.BlockSpec(memory_space=pltpu.HBM)] * 5,
        out_specs=pl.BlockSpec(memory_space=pltpu.VMEM),
        scratch_shapes=[
            pltpu.SMEM(owners.shape, jnp.int32),
            pltpu.SMEM(refresh.shape, jnp.int32),
            pltpu.VMEM(params.shape, BF16),
            pltpu.VMEM((width, width), F32),
            pltpu.VMEM((width, width), BF16),
            pltpu.VMEM((7, width, width), BF16),
            pltpu.VMEM((7, width, width), BF16),
            pltpu.VMEM((nd, 16, 128), BF16),
            pltpu.VMEM((2, pieces, 8 * nh, 128), BF16),
            pltpu.VMEM((nh, 16, 128), BF16),
            pltpu.VMEM((ns, 16, 128), BF16),
            pltpu.VMEM((16, 128), BF16),
            pltpu.VMEM((16, 128), BF16),
            pltpu.VMEM((pieces, 16, 128), BF16),
            pltpu.VMEM((nh, 16, 128), BF16),
            pltpu.VMEM((width, 128), BF16),
            pltpu.VMEM((pieces, 16, 128), F32),
            pltpu.VMEM((nh, 8, 128), F32),
            pltpu.SemaphoreType.DMA((5,)),
            pltpu.SemaphoreType.DMA((9,)),
            pltpu.SemaphoreType.DMA((9,)),
        ],
        compiler_params=pltpu.CompilerParams(
            collective_id=0, has_side_effects=True, vmem_limit_bytes=127 * 2 ** 19
        ),
    )(owners, refresh, grad_parts, statistics, stale_roots)
    new_momentum = 0.9 * momentum + direction
    return params - 0.1 * new_momentum, new_momentum


def solution(mesh):
    rows = P("shard", None)
    body = functools.partial(per_device, mesh.shape["dp"], mesh.shape["shard"])
    return jax.shard_map(
        body,
        mesh=mesh,
        in_specs=(P("dp", "shard", None), rows, rows, rows, rows, P(), P()),
        out_specs=(rows, rows),
        check_vma=False,
    )
```

```python
import functools

import jax
import jax.numpy as jnp
from jax import lax
from jax.experimental import pallas as pl
from jax.experimental.pallas import tpu as pltpu
from jax.sharding import PartitionSpec as P

MESH = pl.DeviceIdType.MESH
F32 = jnp.float32
BF16 = jnp.bfloat16
NT = (((1,), (1,)), ((), ()))
NN = (((1,), (0,)), ((), ()))
SMALL = 2.0 ** -20


def dot(a, b, dims=NN):
    return lax.dot_general(a, b, dims, preferred_element_type=F32)


def halves(value):
    high = value.astype(BF16)
    return high, (value - high.astype(F32)).astype(BF16)


def swap(tiles, part, count):
    size = 128 // count
    out = []
    for q in range(count):
        total = tiles[0] if q == 0 else pltpu.roll(tiles[0], 128 - size * q, 1)
        for p in range(1, count):
            other = tiles[p] if p == q else pltpu.roll(tiles[p], size * (p - q) % 128, 1)
            total = jnp.where(part == p, other, total)
        out.append(total)
    return out


def kernel(
    nd, ns, owners_hbm, refresh_hbm, grad_hbm, stat_hbm, stale_hbm, out_ref,
    owners, refresh, grad_v, stat_v, stale_v, mh, ml, rs_buf, gp, x_send, x_buf, l_send,
    r_send, l_buf, r_buf, lt_v, t_buf, n_buf, local_sem, send_sem, recv_sem,
):
    width = stat_v.shape[0]
    nh = ns // 2
    nz = nh // 2
    groups = width // 128
    pieces = 2 * groups
    nx = groups
    ny = nd // nx
    span = 16 * nz
    d = lax.axis_index("dp")
    s = lax.axis_index("shard")
    x = d % nx
    y = d // nx
    block = s // nh
    t = s % nh
    core = s % 2
    z = t // 2

    def part_of(dp):
        row = dp // nx
        return row % 2 * nx + lax.rem(dp % nx + 2 * (row // 2), nx)

    mine = part_of(d)

    load_grad = pltpu.make_async_copy(grad_hbm.at[0], grad_v, local_sem.at[0])
    load_stat = pltpu.make_async_copy(stat_hbm, stat_v, local_sem.at[1])
    load_stale = pltpu.make_async_copy(stale_hbm, stale_v, local_sem.at[2])
    load_owners = pltpu.make_async_copy(owners_hbm, owners, local_sem.at[3])
    load_refresh = pltpu.make_async_copy(refresh_hbm, refresh, local_sem.at[4])
    load_grad.start()
    load_stat.start()
    load_stale.start()
    load_owners.start()
    load_refresh.start()

    barrier = pltpu.get_barrier_semaphore()

    @pl.loop(1, nd)
    def _(k):
        pl.semaphore_signal(
            barrier, inc=1, device_id=(lax.rem(d + k, nd), s), device_id_type=MESH
        )

    @pl.loop(1, ns)
    def _(k):
        pl.semaphore_signal(
            barrier, inc=1, device_id=(d, lax.rem(s + k, ns)), device_id_type=MESH
        )

    def send(phase, src, dst, dp, shard):
        pltpu.make_async_remote_copy(
            src_ref=src, dst_ref=dst, send_sem=send_sem.at[phase],
            recv_sem=recv_sem.at[phase], device_id=(dp, shard), device_id_type=MESH,
        ).start()

    def whole(phase, ref):
        return pltpu.make_async_remote_copy(
            src_ref=ref, dst_ref=ref, send_sem=send_sem.at[phase],
            recv_sem=recv_sem.at[phase], device_id=(lax.rem(d + 1, nd), s), device_id_type=MESH,
        )

    shifts = [(1, 0), (3, 0), (2, 0), (0, 1), (0, 3), (1, 1), (1, 3)] if nx == 4 else [(0, 1)]
    near = [lax.rem(y + ny - b, ny) * nx + lax.rem(x + nx - a, nx) for a, b in shifts]
    near_from = [lax.rem(y + b, ny) * nx + lax.rem(x + a, nx) for a, b in shifts]

    def send_near(phase, src, dst):
        for other in near:
            send(phase, src, dst, other, s)

    def forward(which):
        send(8, gp.at[core, which], gp.at[core, which], d, s + 1 - 2 * core)

    def grad_piece(which):
        row = pl.multiple_of(which // groups * 16, 16)
        column = pl.multiple_of(which % groups * 128, 128)
        return grad_v.at[pl.ds(row, 16), pl.ds(column, 128)]

    load_grad.wait()
    rs_buf[d] = grad_piece(mine)[...]
    pl.semaphore_wait(barrier, ns + nd - 2)

    @pl.loop(1, nd)
    def _(k):
        other = lax.rem(d + k, nd)
        send(0, grad_piece(part_of(other)), rs_buf.at[d], other, s)

    load_stat.wait()
    tall = 128
    blocks = width // tall

    def row_sums(r, most):
        rows = pl.ds(pl.multiple_of(r * tall, tall), tall)
        return jnp.maximum(most, jnp.sum(jnp.abs(stat_v[rows]), axis=1, keepdims=True))

    most = lax.fori_loop(0, blocks, row_sums, jnp.zeros((tall, 1), F32))
    bound = jnp.max(most, axis=0, keepdims=True)
    inverse = 1.0 / (bound * SMALL)

    @pl.loop(0, blocks)
    def _(r):
        rows = pl.ds(pl.multiple_of(r * tall, tall), tall)
        mh[0, rows], ml[0, rows] = halves((stat_v[rows] * SMALL) * inverse)

    def product(first, second, result, alpha, beta, both):
        total = dot(mh[first], mh[second])
        if both:
            total = total + dot(ml[first], mh[second])
        kept = mh[second].astype(F32) + ml[second].astype(F32)
        mh[result], ml[result] = halves(alpha * kept + beta * total)

    for base in (0, 3, 6):
        product(base, base, base + 1, -0.625, 0.0625, False)
        if base < 6:
            product(base + 1, base + 1, base + 2, 3.125, 1.0, False)
            product(base + 2, base, base + 3, 2.44140625, 1.0, True)

    column = lax.broadcasted_iota(jnp.int32, (64, width), 1)
    line = lax.broadcasted_iota(jnp.int32, (64, width), 0)
    picked = jnp.where(column == line + 64 * mine, 1.0, 0.0)

    def apply(slot, value, alpha, beta):
        total = dot(jnp.concatenate(halves(value), 0), mh[slot], NT)
        return alpha * value + beta * (total[:64] + total[64:])

    left = apply(3, apply(0, picked, 1.25, -0.25), 1.25, -0.25)
    first = apply(6, left, 0.0, 1.0)
    second = apply(6, first, 0.0, 1.0)
    left = 1.25 * left - 0.25 * first
    right = 1.25 * first - 0.25 * second
    right = apply(7, apply(7, right, 1.5625, 1.0), 1.5625, 1.0)
    fresh = (1.25 * left - 0.25 * right) * lax.rsqrt(jnp.sqrt(bound))
    load_stale.wait()
    load_owners.wait()
    load_refresh.wait()
    stale = dot(picked.astype(BF16), stale_v[...], NT)
    flag = jnp.int32(0)
    for f in range(4):
        flag = flag + jnp.where(owners[f] == s, refresh[f // 2], 0)
    chosen = jnp.full((64, width), flag, jnp.int32) > 0
    root = jnp.where(chosen, fresh, stale)

    quarter = lax.broadcasted_iota(jnp.int32, (16, 128), 1) // 32
    half = quarter // 2
    for g in range(groups):
        tiles = [root[16 * q:16 * q + 16, 128 * g:128 * g + 128] for q in range(4)]
        tiles = swap(tiles, quarter, 4)
        for p in range(4):
            x_send[4 * g + p] = tiles[p].astype(BF16)
    x_buf[s] = x_send[t]

    @pl.loop(1, ns)
    def _(k):
        other = lax.rem(s + k, ns)
        send(3, x_send.at[lax.rem(other, nh)], x_buf.at[s], d, other)

    whole(0, rs_buf.at[pl.ds(0, nd - 1)]).wait_recv()
    summed = rs_buf[0].astype(F32)
    for k in range(1, nd):
        summed = summed + rs_buf[k].astype(F32)
    here = pl.ds(pl.multiple_of(z * 16, 16), 16)
    gp[core, mine, here] = (summed * (1.0 / nd)).astype(BF16)

    @pl.loop(1, nz)
    def _(k):
        spot = gp.at[core, mine, here]
        send(1, spot, spot, d, block * nh + lax.rem(t + 2 * k, nh))

    whole(1, gp.at[0, 0, pl.ds(0, span - 16)]).wait_recv()
    spot = gp.at[core, mine]
    for k, other in enumerate(near):
        send(9 + k, spot, spot, other, s)
    forward(mine)

    whole(3, x_buf.at[pl.ds(0, ns - 1)]).wait_recv()

    piece = x_buf[owners[2 * block + 1]]
    r_send[...] = piece
    r_buf[t] = piece

    @pl.loop(1, nh)
    def _(k):
        send(4, r_send, r_buf.at[t], d, block * nh + lax.rem(t + k, nh))

    piece = x_buf[owners[2 * block]]
    l_send[...] = piece
    l_buf[mine] = piece
    send_near(5, l_send, l_buf.at[mine])

    whole(5, l_buf.at[pl.ds(0, pieces - 1)]).wait_recv()
    for k in range(pieces):
        tile = l_buf[k].astype(F32)
        for q in range(4):
            row = q * span + 16 * k
            turned = tile if q == 0 else pltpu.roll(tile, 128 - 32 * q, 1)
            lt_v[row:row + 16] = turned.astype(BF16)

    whole(4, r_buf.at[pl.ds(0, nh - 1)]).wait_recv()
    parts = []
    for g in range(groups):
        tiles = [r_buf[4 * g + p].astype(F32) for p in range(4)]
        parts.append(jnp.concatenate(swap(tiles, quarter, 4), 0))
    right_root = jnp.concatenate(parts, 1).astype(BF16)

    for k, other in enumerate(near_from):
        whole(9 + k, gp.at[0, 0]).wait_recv()
        forward(part_of(other))

    whole(8, gp.at[0]).wait_recv()
    grad = jnp.concatenate([
        jnp.concatenate([gp[c, h * groups + g] for g in range(groups)], 1)
        for c in range(2) for h in range(2)
    ], 0)
    image = dot(right_root, grad, NT).astype(BF16)
    turned = dot(image, lt_v[...])
    turned = jnp.concatenate([turned, jnp.zeros((64, 128), F32)], 0).T
    tile = jnp.where(half == 0, turned[0:16], pltpu.roll(turned[16:32], 64, 1))
    t_buf[mine] = tile
    send_near(6, t_buf.at[mine], t_buf.at[mine])

    def grad_square(k, total):
        tile = gp[k // pieces, k % pieces].astype(F32)
        tile = tile * tile
        return total + jnp.sum(tile.reshape(span // 8, 8, 128), axis=0)

    grad_sq = lax.fori_loop(0, 2 * pieces, grad_square, jnp.zeros((8, 128), F32))
    grad_sum = jnp.sum(jnp.sum(grad_sq, axis=1, keepdims=True), axis=0, keepdims=True)

    whole(6, t_buf.at[pl.ds(0, pieces - 1)]).wait_recv()
    rows = [swap([t_buf[2 * g], t_buf[2 * g + 1]], half, 2) for g in range(groups)]
    square = sum(tile * tile for part in rows for tile in part)
    n_buf[t] = square[:8] + square[8:]

    @pl.loop(1, nh)
    def _(k):
        spot = n_buf.at[t]
        send(7, spot, spot, d, block * nh + lax.rem(t + k, nh))

    whole(7, n_buf.at[pl.ds(0, nh - 1)]).wait_recv()
    square = sum(n_buf[k] for k in range(nh))
    square = jnp.sum(jnp.sum(square, axis=1, keepdims=True), axis=0, keepdims=True)
    scale = jnp.sqrt(grad_sum) * lax.rsqrt(square + 1e-6)
    for g in range(groups):
        for u in range(2):
            out_ref[16 * u:16 * u + 16, 128 * g:128 * g + 128] = rows[g][u] * scale

    whole(0, rs_buf.at[pl.ds(0, nd - 1)]).wait_send()
    whole(1, gp.at[0, 0, pl.ds(0, span - 16)]).wait_send()
    for k in range(pieces - 1):
        whole(9 + k, gp.at[0, 0]).wait_send()
    whole(3, x_buf.at[pl.ds(0, ns - 1)]).wait_send()
    whole(4, r_buf.at[pl.ds(0, nh - 1)]).wait_send()
    whole(5, l_buf.at[pl.ds(0, pieces - 1)]).wait_send()
    whole(6, t_buf.at[pl.ds(0, pieces - 1)]).wait_send()
    whole(7, n_buf.at[pl.ds(0, nh - 1)]).wait_send()
    whole(8, gp.at[0]).wait_send()


def per_device(nd, ns, grad_parts, params, momentum, statistics, stale_roots, owners, refresh):
    width = params.shape[1]
    nh = ns // 2
    pieces = width // 64
    direction = pl.pallas_call(
        functools.partial(kernel, nd, ns),
        out_shape=jax.ShapeDtypeStruct(params.shape, F32),
        in_specs=[pl.BlockSpec(memory_space=pltpu.HBM)] * 5,
        out_specs=pl.BlockSpec(memory_space=pltpu.VMEM),
        scratch_shapes=[
            pltpu.SMEM(owners.shape, jnp.int32),
            pltpu.SMEM(refresh.shape, jnp.int32),
            pltpu.VMEM(params.shape, BF16),
            pltpu.VMEM((width, width), F32),
            pltpu.VMEM((width, width), BF16),
            pltpu.VMEM((8, width, width), BF16),
            pltpu.VMEM((8, width, width), BF16),
            pltpu.VMEM((nd, 16, 128), BF16),
            pltpu.VMEM((2, pieces, 8 * nh, 128), BF16),
            pltpu.VMEM((nh, 16, 128), BF16),
            pltpu.VMEM((ns, 16, 128), BF16),
            pltpu.VMEM((16, 128), BF16),
            pltpu.VMEM((16, 128), BF16),
            pltpu.VMEM((pieces, 16, 128), BF16),
            pltpu.VMEM((nh, 16, 128), BF16),
            pltpu.VMEM((width, 128), BF16),
            pltpu.VMEM((pieces, 16, 128), F32),
            pltpu.VMEM((nh, 8, 128), F32),
            pltpu.SemaphoreType.DMA((5,)),
            pltpu.SemaphoreType.DMA((8 + pieces,)),
            pltpu.SemaphoreType.DMA((8 + pieces,)),
        ],
        compiler_params=pltpu.CompilerParams(
            collective_id=0, has_side_effects=True, vmem_limit_bytes=63 * 2 ** 20
        ),
    )(owners, refresh, grad_parts, statistics, stale_roots)
    new_momentum = 0.9 * momentum + direction
    return params - 0.1 * new_momentum, new_momentum


def solution(mesh):
    rows = P("shard", None)
    body = functools.partial(per_device, mesh.shape["dp"], mesh.shape["shard"])
    return jax.shard_map(
        body,
        mesh=mesh,
        in_specs=(P("dp", "shard", None), rows, rows, rows, rows, P(), P()),
        out_specs=(rows, rows),
        check_vma=False,
    )
```

```python
import functools

import jax
import jax.numpy as jnp
from jax import lax
from jax.experimental import pallas as pl
from jax.experimental.pallas import tpu as pltpu
from jax.sharding import PartitionSpec as P

MESH = pl.DeviceIdType.MESH
F32 = jnp.float32
BF16 = jnp.bfloat16
NT = (((1,), (1,)), ((), ()))
NN = (((1,), (0,)), ((), ()))
SMALL = 2.0 ** -20


def dot(a, b, dims=NN):
    return lax.dot_general(a, b, dims, preferred_element_type=F32)


def halves(value):
    high = value.astype(BF16)
    return high, (value - high.astype(F32)).astype(BF16)


def swap(tiles, part, count):
    size = 128 // count
    out = []
    for q in range(count):
        total = tiles[0] if q == 0 else pltpu.roll(tiles[0], 128 - size * q, 1)
        for p in range(1, count):
            other = tiles[p] if p == q else pltpu.roll(tiles[p], size * (p - q) % 128, 1)
            total = jnp.where(part == p, other, total)
        out.append(total)
    return out


def kernel(
    nd, ns, owners_hbm, refresh_hbm, grad_hbm, stat_hbm, stale_hbm, out_ref,
    owners, refresh, grad_v, stat_v, stale_v, mh, ml, rs_buf, gp, x_send, x_buf, l_send,
    r_send, l_buf, r_buf, lt_v, t_buf, n_buf, local_sem, send_sem, recv_sem,
):
    width = stat_v.shape[0]
    nh = ns // 2
    nz = nh // 2
    groups = width // 128
    pieces = 2 * groups
    nx = groups
    ny = nd // nx
    span = 16 * nz
    d = lax.axis_index("dp")
    s = lax.axis_index("shard")
    x = d % nx
    y = d // nx
    block = s // nh
    t = s % nh
    core = s % 2
    z = t // 2

    def part_of(dp):
        row = dp // nx
        return row % 2 * nx + lax.rem(dp % nx + 2 * (row // 2), nx)

    mine = part_of(d)

    load_grad = pltpu.make_async_copy(grad_hbm.at[0], grad_v, local_sem.at[0])
    load_stat = pltpu.make_async_copy(stat_hbm, stat_v, local_sem.at[1])
    load_stale = pltpu.make_async_copy(stale_hbm, stale_v, local_sem.at[2])
    load_owners = pltpu.make_async_copy(owners_hbm, owners, local_sem.at[3])
    load_refresh = pltpu.make_async_copy(refresh_hbm, refresh, local_sem.at[4])
    load_stat.start()
    load_grad.start()

    barrier = pltpu.get_barrier_semaphore()

    def far(k, count):
        return (count // 2 + (k + 1) // 2 * (1 - 2 * (k % 2))) % count

    def over_groups(k):
        return (y + far(k // nx, ny)) % ny * nx + (x + far(k % nx, nx)) % nx

    def over_block(k):
        return block * nh + (z + far(k // 2, nz)) % nz * 2 + (core + 1 - k % 2) % 2

    def over_shards(k):
        where = (block + 1 - k % 4 // 2) % 2
        return where * nh + (z + far(k // 4, nz)) % nz * 2 + (core + 1 - k % 2) % 2

    @pl.loop(0, nd - 1)
    def _(k):
        pl.semaphore_signal(barrier, inc=1, device_id=(over_groups(k), s), device_id_type=MESH)

    @pl.loop(0, ns - 1)
    def _(k):
        pl.semaphore_signal(barrier, inc=1, device_id=(d, over_shards(k)), device_id_type=MESH)

    load_stale.start()
    load_owners.start()
    load_refresh.start()

    def send(phase, src, dst, dp, shard):
        pltpu.make_async_remote_copy(
            src_ref=src, dst_ref=dst, send_sem=send_sem.at[phase],
            recv_sem=recv_sem.at[phase], device_id=(dp, shard), device_id_type=MESH,
        ).start()

    def whole(phase, ref):
        return pltpu.make_async_remote_copy(
            src_ref=ref, dst_ref=ref, send_sem=send_sem.at[phase],
            recv_sem=recv_sem.at[phase], device_id=(lax.rem(d + 1, nd), s), device_id_type=MESH,
        )

    shifts = [(1, 1), (1, 3), (2, 0), (0, 1), (0, 3), (1, 0), (3, 0)] if nx == 4 else [(0, 1)]
    near = [lax.rem(y + ny - b, ny) * nx + lax.rem(x + nx - a, nx) for a, b in shifts]
    near_from = [lax.rem(y + b, ny) * nx + lax.rem(x + a, nx) for a, b in shifts]

    def send_near(phase, src, dst):
        for other in near:
            send(phase, src, dst, other, s)

    def forward(which):
        send(8, gp.at[core, which], gp.at[core, which], d, s + 1 - 2 * core)

    def grad_piece(which):
        row = pl.multiple_of(which // groups * 16, 16)
        column = pl.multiple_of(which % groups * 128, 128)
        return grad_v.at[pl.ds(row, 16), pl.ds(column, 128)]

    load_grad.wait()
    rs_buf[d] = grad_piece(mine)[...]
    pl.semaphore_wait(barrier, ns + nd - 2)

    @pl.loop(0, nd - 1)
    def _(k):
        other = over_groups(k)
        send(0, grad_piece(part_of(other)), rs_buf.at[d], other, s)

    load_stat.wait()
    tall = 128
    blocks = width // tall

    def row_sums(r, most):
        rows = pl.ds(pl.multiple_of(r * tall, tall), tall)
        return jnp.maximum(most, jnp.sum(jnp.abs(stat_v[rows]), axis=1, keepdims=True))

    most = lax.fori_loop(0, blocks, row_sums, jnp.zeros((tall, 1), F32))
    bound = jnp.max(most, axis=0, keepdims=True)
    inverse = 1.0 / (bound * SMALL)

    @pl.loop(0, blocks)
    def _(r):
        rows = pl.ds(pl.multiple_of(r * tall, tall), tall)
        mh[0, rows], ml[0, rows] = halves((stat_v[rows] * SMALL) * inverse)

    def product(first, second, result, alpha, beta, both):
        total = dot(mh[first], mh[second])
        if both:
            total = total + dot(ml[first], mh[second])
        kept = mh[second].astype(F32) + ml[second].astype(F32)
        mh[result], ml[result] = halves(alpha * kept + beta * total)

    for base in (0, 3, 6):
        product(base, base, base + 1, -0.625, 0.0625, False)
        if base < 6:
            product(base + 1, base + 1, base + 2, 3.125, 1.0, False)
            product(base + 2, base, base + 3, 2.44140625, 1.0, True)

    column = lax.broadcasted_iota(jnp.int32, (64, width), 1)
    line = lax.broadcasted_iota(jnp.int32, (64, width), 0)
    picked = jnp.where(column == line + 64 * mine, 1.0, 0.0)

    def apply(slot, value, alpha, beta):
        total = dot(jnp.concatenate(halves(value), 0), mh[slot], NT)
        return alpha * value + beta * (total[:64] + total[64:])

    left = apply(3, apply(0, picked, 1.25, -0.25), 1.25, -0.25)
    first = apply(6, left, 0.0, 1.0)
    second = apply(6, first, 0.0, 1.0)
    left = 1.25 * left - 0.25 * first
    right = 1.25 * first - 0.25 * second
    right = apply(7, apply(7, right, 1.5625, 1.0), 1.5625, 1.0)
    fresh = (1.25 * left - 0.25 * right) * lax.rsqrt(jnp.sqrt(bound))
    load_stale.wait()
    load_owners.wait()
    load_refresh.wait()
    stale = dot(picked.astype(BF16), stale_v[...], NT)
    flag = jnp.int32(0)
    for f in range(4):
        flag = flag + jnp.where(owners[f] == s, refresh[f // 2], 0)
    chosen = jnp.full((64, width), flag, jnp.int32) > 0
    root = jnp.where(chosen, fresh, stale)

    quarter = lax.broadcasted_iota(jnp.int32, (16, 128), 1) // 32
    half = quarter // 2
    for g in range(groups):
        tiles = [root[16 * q:16 * q + 16, 128 * g:128 * g + 128] for q in range(4)]
        tiles = swap(tiles, quarter, 4)
        for p in range(4):
            x_send[4 * g + p] = tiles[p].astype(BF16)
    x_buf[s] = x_send[t]

    whole(0, rs_buf.at[pl.ds(0, nd - 1)]).wait_recv()
    summed = rs_buf[0].astype(F32)
    for k in range(1, nd):
        summed = summed + rs_buf[k].astype(F32)
    here = pl.ds(pl.multiple_of(z * 16, 16), 16)
    gp[core, mine, here] = (summed * (1.0 / nd)).astype(BF16)

    @pl.loop(0, nz - 1)
    def _(k):
        spot = gp.at[core, mine, here]
        send(1, spot, spot, d, block * nh + (z + far(k, nz)) % nz * 2 + core)

    @pl.loop(0, ns - 1)
    def _(k):
        other = over_shards(k)
        send(3, x_send.at[lax.rem(other, nh)], x_buf.at[s], d, other)

    whole(1, gp.at[0, 0, pl.ds(0, span - 16)]).wait_recv()
    spot = gp.at[core, mine]
    for k, other in enumerate(near):
        send(9 + k, spot, spot, other, s)
    forward(mine)

    whole(3, x_buf.at[pl.ds(0, ns - 1)]).wait_recv()

    piece = x_buf[owners[2 * block + 1]]
    r_send[...] = piece
    r_buf[t] = piece

    @pl.loop(0, nh - 1)
    def _(k):
        send(4, r_send, r_buf.at[t], d, over_block(k))

    piece = x_buf[owners[2 * block]]
    l_send[...] = piece
    l_buf[mine] = piece
    send_near(5, l_send, l_buf.at[mine])

    whole(5, l_buf.at[pl.ds(0, pieces - 1)]).wait_recv()
    for k in range(pieces):
        tile = l_buf[k].astype(F32)
        for q in range(4):
            row = q * span + 16 * k
            turned = tile if q == 0 else pltpu.roll(tile, 128 - 32 * q, 1)
            lt_v[row:row + 16] = turned.astype(BF16)

    whole(4, r_buf.at[pl.ds(0, nh - 1)]).wait_recv()
    parts = []
    for g in range(groups):
        tiles = [r_buf[4 * g + p].astype(F32) for p in range(4)]
        parts.append(jnp.concatenate(swap(tiles, quarter, 4), 0))
    right_root = jnp.concatenate(parts, 1).astype(BF16)

    for k in reversed(range(pieces - 1)):
        whole(9 + k, gp.at[0, 0]).wait_recv()
        forward(part_of(near_from[k]))

    def tile_part(c):
        grad = jnp.concatenate([
            jnp.concatenate([gp[c, h * groups + g] for g in range(groups)], 1) for h in range(2)
        ], 0)
        rows = pl.ds(pl.multiple_of(c * 2 * span, 2 * span), 2 * span)
        return dot(dot(right_root, grad, NT).astype(BF16), lt_v[rows])

    turned = tile_part(core)
    whole(8, gp.at[0]).wait_recv()
    other = tile_part(1 - core)
    turned = turned + other
    turned = jnp.concatenate([turned, jnp.zeros((64, 128), F32)], 0).T
    tile = jnp.where(half == 0, turned[0:16], pltpu.roll(turned[16:32], 64, 1))
    t_buf[mine] = tile.astype(BF16)
    send_near(6, t_buf.at[mine], t_buf.at[mine])

    def grad_square(k, total):
        tile = gp[k // pieces, k % pieces].astype(F32)
        tile = tile * tile
        return total + jnp.sum(tile.reshape(span // 8, 8, 128), axis=0)

    grad_sq = lax.fori_loop(0, 2 * pieces, grad_square, jnp.zeros((8, 128), F32))
    grad_sum = jnp.sum(jnp.sum(grad_sq, axis=1, keepdims=True), axis=0, keepdims=True)

    whole(6, t_buf.at[pl.ds(0, pieces - 1)]).wait_recv()
    rows = [
        swap([t_buf[2 * g].astype(F32), t_buf[2 * g + 1].astype(F32)], half, 2)
        for g in range(groups)
    ]
    square = sum(tile * tile for part in rows for tile in part)
    n_buf[t] = square[:8] + square[8:]

    @pl.loop(0, nh - 1)
    def _(k):
        spot = n_buf.at[t]
        send(7, spot, spot, d, over_block(k))

    whole(7, n_buf.at[pl.ds(0, nh - 1)]).wait_recv()
    square = sum(n_buf[k] for k in range(nh))
    square = jnp.sum(jnp.sum(square, axis=1, keepdims=True), axis=0, keepdims=True)
    scale = jnp.sqrt(grad_sum) * lax.rsqrt(square + 1e-6)
    for g in range(groups):
        for u in range(2):
            out_ref[16 * u:16 * u + 16, 128 * g:128 * g + 128] = rows[g][u] * scale

    whole(0, rs_buf.at[pl.ds(0, nd - 1)]).wait_send()
    whole(1, gp.at[0, 0, pl.ds(0, span - 16)]).wait_send()
    for k in range(pieces - 1):
        whole(9 + k, gp.at[0, 0]).wait_send()
    whole(3, x_buf.at[pl.ds(0, ns - 1)]).wait_send()
    whole(4, r_buf.at[pl.ds(0, nh - 1)]).wait_send()
    whole(5, l_buf.at[pl.ds(0, pieces - 1)]).wait_send()
    whole(6, t_buf.at[pl.ds(0, pieces - 1)]).wait_send()
    whole(7, n_buf.at[pl.ds(0, nh - 1)]).wait_send()
    whole(8, gp.at[0]).wait_send()


def per_device(nd, ns, grad_parts, params, momentum, statistics, stale_roots, owners, refresh):
    width = params.shape[1]
    nh = ns // 2
    pieces = width // 64
    direction = pl.pallas_call(
        functools.partial(kernel, nd, ns),
        out_shape=jax.ShapeDtypeStruct(params.shape, F32),
        in_specs=[pl.BlockSpec(memory_space=pltpu.HBM)] * 5,
        out_specs=pl.BlockSpec(memory_space=pltpu.VMEM),
        scratch_shapes=[
            pltpu.SMEM(owners.shape, jnp.int32),
            pltpu.SMEM(refresh.shape, jnp.int32),
            pltpu.VMEM(params.shape, BF16),
            pltpu.VMEM((width, width), F32),
            pltpu.VMEM((width, width), BF16),
            pltpu.VMEM((8, width, width), BF16),
            pltpu.VMEM((8, width, width), BF16),
            pltpu.VMEM((nd, 16, 128), BF16),
            pltpu.VMEM((2, pieces, 8 * nh, 128), BF16),
            pltpu.VMEM((nh, 16, 128), BF16),
            pltpu.VMEM((ns, 16, 128), BF16),
            pltpu.VMEM((16, 128), BF16),
            pltpu.VMEM((16, 128), BF16),
            pltpu.VMEM((pieces, 16, 128), BF16),
            pltpu.VMEM((nh, 16, 128), BF16),
            pltpu.VMEM((width, 128), BF16),
            pltpu.VMEM((pieces, 16, 128), BF16),
            pltpu.VMEM((nh, 8, 128), F32),
            pltpu.SemaphoreType.DMA((5,)),
            pltpu.SemaphoreType.DMA((8 + pieces,)),
            pltpu.SemaphoreType.DMA((8 + pieces,)),
        ],
        compiler_params=pltpu.CompilerParams(
            collective_id=0, has_side_effects=True, vmem_limit_bytes=63 * 2 ** 20
        ),
    )(owners, refresh, grad_parts, statistics, stale_roots)
    new_momentum = 0.9 * momentum + direction
    return params - 0.1 * new_momentum, new_momentum


def solution(mesh):
    rows = P("shard", None)
    body = functools.partial(per_device, mesh.shape["dp"], mesh.shape["shard"])
    return jax.shard_map(
        body,
        mesh=mesh,
        in_specs=(P("dp", "shard", None), rows, rows, rows, rows, P(), P()),
        out_specs=(rows, rows),
        check_vma=False,
    )
```

```python
import functools

import jax
import jax.numpy as jnp
from jax import lax
from jax.experimental import pallas as pl
from jax.experimental.pallas import tpu as pltpu
from jax.sharding import PartitionSpec as P

MESH = pl.DeviceIdType.MESH
F32 = jnp.float32
BF16 = jnp.bfloat16
NT = (((1,), (1,)), ((), ()))
NN = (((1,), (0,)), ((), ()))
SMALL = 2.0 ** -20


def dot(a, b, dims=NN):
    return lax.dot_general(a, b, dims, preferred_element_type=F32)


def halves(value):
    high = value.astype(BF16)
    return high, (value - high.astype(F32)).astype(BF16)


def swap(tiles, part, count):
    size = 128 // count
    out = []
    for q in range(count):
        total = tiles[0] if q == 0 else pltpu.roll(tiles[0], 128 - size * q, 1)
        for p in range(1, count):
            other = tiles[p] if p == q else pltpu.roll(tiles[p], size * (p - q) % 128, 1)
            total = jnp.where(part == p, other, total)
        out.append(total)
    return out


def kernel(
    nd, ns, owners_hbm, refresh_hbm, grad_hbm, stat_hbm, stale_hbm, out_ref,
    owners, refresh, grad_v, stat_v, stale_v, mh, ml, rs_buf, gp, x_send, x_buf, l_send,
    r_send, l_buf, r_buf, lt_v, t_buf, n_buf, local_sem, send_sem, recv_sem,
):
    width = stat_v.shape[0]
    nh = ns // 2
    nz = nh // 2
    groups = width // 128
    pieces = 2 * groups
    nx = groups
    ny = nd // nx
    span = 16 * nz
    d = lax.axis_index("dp")
    s = lax.axis_index("shard")
    x = d % nx
    y = d // nx
    block = s // nh
    t = s % nh
    core = s % 2
    z = t // 2

    def part_of(dp):
        row = dp // nx
        return row % 2 * nx + lax.rem(dp % nx + 2 * (row // 2), nx)

    mine = part_of(d)

    load_grad = pltpu.make_async_copy(grad_hbm.at[0], grad_v, local_sem.at[0])
    load_stat = pltpu.make_async_copy(stat_hbm, stat_v, local_sem.at[1])
    load_stale = pltpu.make_async_copy(stale_hbm, stale_v, local_sem.at[2])
    load_owners = pltpu.make_async_copy(owners_hbm, owners, local_sem.at[3])
    load_refresh = pltpu.make_async_copy(refresh_hbm, refresh, local_sem.at[4])
    load_stat.start()
    load_grad.start()

    barrier = pltpu.get_barrier_semaphore()

    def far(k, count):
        return (count // 2 + (k + 1) // 2 * (1 - 2 * (k % 2))) % count

    def over_groups(k):
        return (y + far(k // nx, ny)) % ny * nx + (x + far(k % nx, nx)) % nx

    def over_block(k):
        return block * nh + (z + far(k // 2, nz)) % nz * 2 + (core + 1 - k % 2) % 2

    def over_shards(k):
        where = (block + 1 - k % 4 // 2) % 2
        return where * nh + (z + far(k // 4, nz)) % nz * 2 + (core + 1 - k % 2) % 2

    @pl.loop(0, nd - 1)
    def _(k):
        pl.semaphore_signal(barrier, inc=1, device_id=(over_groups(k), s), device_id_type=MESH)

    @pl.loop(0, ns - 1)
    def _(k):
        pl.semaphore_signal(barrier, inc=1, device_id=(d, over_shards(k)), device_id_type=MESH)

    load_stale.start()
    load_owners.start()
    load_refresh.start()

    def send(phase, src, dst, dp, shard):
        pltpu.make_async_remote_copy(
            src_ref=src, dst_ref=dst, send_sem=send_sem.at[phase],
            recv_sem=recv_sem.at[phase], device_id=(dp, shard), device_id_type=MESH,
        ).start()

    def whole(phase, ref):
        return pltpu.make_async_remote_copy(
            src_ref=ref, dst_ref=ref, send_sem=send_sem.at[phase],
            recv_sem=recv_sem.at[phase], device_id=(lax.rem(d + 1, nd), s), device_id_type=MESH,
        )

    shifts = [(1, 1), (1, 3), (2, 0), (0, 1), (0, 3), (1, 0), (3, 0)] if nx == 4 else [(0, 1)]
    near = [lax.rem(y + ny - b, ny) * nx + lax.rem(x + nx - a, nx) for a, b in shifts]
    near_from = [lax.rem(y + b, ny) * nx + lax.rem(x + a, nx) for a, b in shifts]

    def send_near(phase, src, dst):
        for other in near:
            send(phase, src, dst, other, s)

    def forward(which):
        send(8, gp.at[core, which], gp.at[core, which], d, s + 1 - 2 * core)

    def grad_piece(which):
        row = pl.multiple_of(which // groups * 16, 16)
        column = pl.multiple_of(which % groups * 128, 128)
        return grad_v.at[pl.ds(row, 16), pl.ds(column, 128)]

    load_grad.wait()
    rs_buf[d] = grad_piece(mine)[...]
    pl.semaphore_wait(barrier, ns + nd - 2)

    @pl.loop(0, nd - 1)
    def _(k):
        other = over_groups(k)
        send(0, grad_piece(part_of(other)), rs_buf.at[d], other, s)

    load_stat.wait()
    most = jnp.sum(jnp.abs(stat_v[...]), axis=1, keepdims=True)
    bound = jnp.max(most, axis=0, keepdims=True)
    inverse = 1.0 / (bound * SMALL)
    mh[0], ml[0] = halves((stat_v[...] * SMALL) * inverse)
    load_stale.wait()
    load_owners.wait()
    load_refresh.wait()

    def product(first, second, result, alpha, beta, both):
        total = dot(mh[first], mh[second])
        if both:
            total = total + dot(ml[first], mh[second])
        kept = mh[second].astype(F32) + ml[second].astype(F32)
        mh[result], ml[result] = halves(alpha * kept + beta * total)

    for base in (0, 3, 6):
        product(base, base, base + 1, -0.625, 0.0625, False)
        if base < 6:
            product(base + 1, base + 1, base + 2, 3.125, 1.0, False)
            product(base + 2, base, base + 3, 2.44140625, 1.0, True)

    column = lax.broadcasted_iota(jnp.int32, (64, width), 1)
    line = lax.broadcasted_iota(jnp.int32, (64, width), 0)
    picked = jnp.where(column == line + 64 * mine, 1.0, 0.0)

    def apply(slot, value, alpha, beta):
        total = dot(jnp.concatenate(halves(value), 0), mh[slot], NT)
        return alpha * value + beta * (total[:64] + total[64:])

    left = apply(3, apply(0, picked, 1.25, -0.25), 1.25, -0.25)
    first = apply(6, left, 0.0, 1.0)
    second = apply(6, first, 0.0, 1.0)
    left = 1.25 * left - 0.25 * first
    right = 1.25 * first - 0.25 * second
    right = apply(7, apply(7, right, 1.5625, 1.0), 1.5625, 1.0)
    fresh = (1.25 * left - 0.25 * right) * lax.rsqrt(jnp.sqrt(bound))
    stale = dot(picked.astype(BF16), stale_v[...], NT)
    flag = jnp.int32(0)
    for f in range(4):
        flag = flag + jnp.where(owners[f] == s, refresh[f // 2], 0)
    chosen = jnp.full((64, width), flag, jnp.int32) > 0
    root = jnp.where(chosen, fresh, stale)

    quarter = lax.broadcasted_iota(jnp.int32, (16, 128), 1) // 32
    half = quarter // 2
    for g in range(groups):
        tiles = [root[16 * q:16 * q + 16, 128 * g:128 * g + 128] for q in range(4)]
        tiles = swap(tiles, quarter, 4)
        for p in range(4):
            x_send[4 * g + p] = tiles[p].astype(BF16)
    x_buf[s] = x_send[t]

    whole(0, rs_buf.at[pl.ds(0, nd - 1)]).wait_recv()
    summed = rs_buf[0].astype(F32)
    for k in range(1, nd):
        summed = summed + rs_buf[k].astype(F32)
    here = pl.ds(pl.multiple_of(z * 16, 16), 16)
    gp[core, mine, here] = (summed * (1.0 / nd)).astype(BF16)

    @pl.loop(0, nz - 1)
    def _(k):
        spot = gp.at[core, mine, here]
        send(1, spot, spot, d, block * nh + (z + far(k, nz)) % nz * 2 + core)

    @pl.loop(0, ns - 1)
    def _(k):
        other = over_shards(k)
        send(3, x_send.at[lax.rem(other, nh)], x_buf.at[s], d, other)

    whole(1, gp.at[0, 0, pl.ds(0, span - 16)]).wait_recv()
    spot = gp.at[core, mine]
    for k, other in enumerate(near):
        send(9 + k, spot, spot, other, s)
    forward(mine)

    whole(3, x_buf.at[pl.ds(0, ns - 1)]).wait_recv()

    piece = x_buf[owners[2 * block + 1]]
    r_send[...] = piece
    r_buf[t] = piece

    @pl.loop(0, nh - 1)
    def _(k):
        send(4, r_send, r_buf.at[t], d, over_block(k))

    piece = x_buf[owners[2 * block]]
    l_send[...] = piece
    l_buf[mine] = piece
    send_near(5, l_send, l_buf.at[mine])

    whole(5, l_buf.at[pl.ds(0, pieces - 1)]).wait_recv()
    for k in range(pieces):
        tile = l_buf[k].astype(F32)
        for q in range(4):
            row = q * span + 16 * k
            turned = tile if q == 0 else pltpu.roll(tile, 128 - 32 * q, 1)
            lt_v[row:row + 16] = turned.astype(BF16)

    whole(4, r_buf.at[pl.ds(0, nh - 1)]).wait_recv()
    parts = []
    for g in range(groups):
        tiles = [r_buf[4 * g + p].astype(F32) for p in range(4)]
        parts.append(jnp.concatenate(swap(tiles, quarter, 4), 0))
    right_root = jnp.concatenate(parts, 1).astype(BF16)

    for k in reversed(range(pieces - 1)):
        whole(9 + k, gp.at[0, 0]).wait_recv()
        forward(part_of(near_from[k]))

    def tile_part(c):
        grad = jnp.concatenate([
            jnp.concatenate([gp[c, h * groups + g] for g in range(groups)], 1) for h in range(2)
        ], 0)
        rows = pl.ds(pl.multiple_of(c * 2 * span, 2 * span), 2 * span)
        return dot(dot(right_root, grad, NT).astype(BF16), lt_v[rows])

    turned = tile_part(core)
    whole(8, gp.at[0]).wait_recv()
    other = tile_part(1 - core)
    turned = turned + other
    turned = jnp.concatenate([turned, jnp.zeros((64, 128), F32)], 0).T
    tile = jnp.where(half == 0, turned[0:16], pltpu.roll(turned[16:32], 64, 1))
    t_buf[mine] = tile.astype(BF16)
    send_near(6, t_buf.at[mine], t_buf.at[mine])

    def grad_square(k, total):
        tile = gp[k // pieces, k % pieces].astype(F32)
        tile = tile * tile
        return total + jnp.sum(tile.reshape(span // 8, 8, 128), axis=0)

    grad_sq = lax.fori_loop(0, 2 * pieces, grad_square, jnp.zeros((8, 128), F32))
    grad_sum = jnp.sum(jnp.sum(grad_sq, axis=1, keepdims=True), axis=0, keepdims=True)

    whole(6, t_buf.at[pl.ds(0, pieces - 1)]).wait_recv()
    rows = [
        swap([t_buf[2 * g].astype(F32), t_buf[2 * g + 1].astype(F32)], half, 2)
        for g in range(groups)
    ]
    square = sum(tile * tile for part in rows for tile in part)
    n_buf[t] = square[:8] + square[8:]

    @pl.loop(0, nh - 1)
    def _(k):
        spot = n_buf.at[t]
        send(7, spot, spot, d, over_block(k))

    whole(7, n_buf.at[pl.ds(0, nh - 1)]).wait_recv()
    square = sum(n_buf[k] for k in range(nh))
    square = jnp.sum(jnp.sum(square, axis=1, keepdims=True), axis=0, keepdims=True)
    scale = jnp.sqrt(grad_sum) * lax.rsqrt(square + 1e-6)
    for g in range(groups):
        for u in range(2):
            out_ref[16 * u:16 * u + 16, 128 * g:128 * g + 128] = rows[g][u] * scale

    whole(0, rs_buf.at[pl.ds(0, nd - 1)]).wait_send()
    whole(1, gp.at[0, 0, pl.ds(0, span - 16)]).wait_send()
    for k in range(pieces - 1):
        whole(9 + k, gp.at[0, 0]).wait_send()
    whole(3, x_buf.at[pl.ds(0, ns - 1)]).wait_send()
    whole(4, r_buf.at[pl.ds(0, nh - 1)]).wait_send()
    whole(5, l_buf.at[pl.ds(0, pieces - 1)]).wait_send()
    whole(6, t_buf.at[pl.ds(0, pieces - 1)]).wait_send()
    whole(7, n_buf.at[pl.ds(0, nh - 1)]).wait_send()
    whole(8, gp.at[0]).wait_send()


def per_device(nd, ns, grad_parts, params, momentum, statistics, stale_roots, owners, refresh):
    width = params.shape[1]
    nh = ns // 2
    pieces = width // 64
    direction = pl.pallas_call(
        functools.partial(kernel, nd, ns),
        out_shape=jax.ShapeDtypeStruct(params.shape, F32),
        in_specs=[pl.BlockSpec(memory_space=pltpu.HBM)] * 5,
        out_specs=pl.BlockSpec(memory_space=pltpu.VMEM),
        scratch_shapes=[
            pltpu.SMEM(owners.shape, jnp.int32),
            pltpu.SMEM(refresh.shape, jnp.int32),
            pltpu.VMEM(params.shape, BF16),
            pltpu.VMEM((width, width), F32),
            pltpu.VMEM((width, width), BF16),
            pltpu.VMEM((8, width, width), BF16),
            pltpu.VMEM((8, width, width), BF16),
            pltpu.VMEM((nd, 16, 128), BF16),
            pltpu.VMEM((2, pieces, 8 * nh, 128), BF16),
            pltpu.VMEM((nh, 16, 128), BF16),
            pltpu.VMEM((ns, 16, 128), BF16),
            pltpu.VMEM((16, 128), BF16),
            pltpu.VMEM((16, 128), BF16),
            pltpu.VMEM((pieces, 16, 128), BF16),
            pltpu.VMEM((nh, 16, 128), BF16),
            pltpu.VMEM((width, 128), BF16),
            pltpu.VMEM((pieces, 16, 128), BF16),
            pltpu.VMEM((nh, 8, 128), F32),
            pltpu.SemaphoreType.DMA((5,)),
            pltpu.SemaphoreType.DMA((8 + pieces,)),
            pltpu.SemaphoreType.DMA((8 + pieces,)),
        ],
        compiler_params=pltpu.CompilerParams(
            collective_id=0, has_side_effects=True, vmem_limit_bytes=63 * 2 ** 20
        ),
    )(owners, refresh, grad_parts, statistics, stale_roots)
    new_momentum = 0.9 * momentum + direction
    return params - 0.1 * new_momentum, new_momentum


def solution(mesh):
    rows = P("shard", None)
    body = functools.partial(per_device, mesh.shape["dp"], mesh.shape["shard"])
    return jax.shard_map(
        body,
        mesh=mesh,
        in_specs=(P("dp", "shard", None), rows, rows, rows, rows, P(), P()),
        out_specs=(rows, rows),
        check_vma=False,
    )
```

```python
import functools

import jax
import jax.numpy as jnp
from jax import lax
from jax.experimental import pallas as pl
from jax.experimental.pallas import tpu as pltpu
from jax.sharding import PartitionSpec as P

MESH = pl.DeviceIdType.MESH
F32 = jnp.float32
BF16 = jnp.bfloat16
NT = (((1,), (1,)), ((), ()))
NN = (((1,), (0,)), ((), ()))
SMALL = 2.0 ** -20


def dot(a, b, dims=NN):
    return lax.dot_general(a, b, dims, preferred_element_type=F32)


def halves(value):
    high = value.astype(BF16)
    return high, (value - high.astype(F32)).astype(BF16)


def swap(tiles, part, count):
    size = 128 // count
    out = []
    for q in range(count):
        total = tiles[0] if q == 0 else pltpu.roll(tiles[0], 128 - size * q, 1)
        for p in range(1, count):
            other = tiles[p] if p == q else pltpu.roll(tiles[p], size * (p - q) % 128, 1)
            total = jnp.where(part == p, other, total)
        out.append(total)
    return out


def kernel(
    nd, ns, owners_hbm, refresh_hbm, grad_hbm, stat_hbm, stale_hbm, out_ref,
    owners, refresh, grad_v, stat_v, stale_v, mh, ml, rs_buf, gp, x_send, x_buf, l_send,
    r_send, l_buf, r_buf, lt_v, t_buf, n_buf, local_sem, send_sem, recv_sem,
):
    width = stat_v.shape[0]
    nh = ns // 2
    nz = nh // 2
    groups = width // 128
    pieces = 2 * groups
    nx = groups
    ny = nd // nx
    span = 16 * nz
    d = lax.axis_index("dp")
    s = lax.axis_index("shard")
    x = d % nx
    y = d // nx
    block = s // nh
    t = s % nh
    core = s % 2
    z = t // 2

    def part_of(dp):
        row = dp // nx
        return row % 2 * nx + lax.rem(dp % nx + 2 * (row // 2), nx)

    mine = part_of(d)

    load_grad = pltpu.make_async_copy(grad_hbm.at[0], grad_v, local_sem.at[0])
    load_stat = pltpu.make_async_copy(stat_hbm, stat_v, local_sem.at[1])
    load_stale = pltpu.make_async_copy(stale_hbm, stale_v, local_sem.at[2])
    load_owners = pltpu.make_async_copy(owners_hbm, owners, local_sem.at[3])
    load_refresh = pltpu.make_async_copy(refresh_hbm, refresh, local_sem.at[4])
    load_stat.start()
    load_grad.start()

    barrier = pltpu.get_barrier_semaphore()

    def far(k, count):
        return (count // 2 + (k + 1) // 2 * (1 - 2 * (k % 2))) % count

    def over_groups(k):
        return (y + far(k // nx, ny)) % ny * nx + (x + far(k % nx, nx)) % nx

    def over_block(k):
        return block * nh + (z + far(k // 2, nz)) % nz * 2 + (core + 1 - k % 2) % 2

    def over_shards(k):
        where = (block + 1 - k % 4 // 2) % 2
        return where * nh + (z + far(k // 4, nz)) % nz * 2 + (core + 1 - k % 2) % 2

    @pl.loop(0, nd - 1)
    def _(k):
        pl.semaphore_signal(barrier, inc=1, device_id=(over_groups(k), s), device_id_type=MESH)

    @pl.loop(0, ns - 1)
    def _(k):
        pl.semaphore_signal(barrier, inc=1, device_id=(d, over_shards(k)), device_id_type=MESH)

    load_stale.start()
    load_owners.start()
    load_refresh.start()

    def send(phase, src, dst, dp, shard):
        pltpu.make_async_remote_copy(
            src_ref=src, dst_ref=dst, send_sem=send_sem.at[phase],
            recv_sem=recv_sem.at[phase], device_id=(dp, shard), device_id_type=MESH,
        ).start()

    def whole(phase, ref):
        return pltpu.make_async_remote_copy(
            src_ref=ref, dst_ref=ref, send_sem=send_sem.at[phase],
            recv_sem=recv_sem.at[phase], device_id=(lax.rem(d + 1, nd), s), device_id_type=MESH,
        )

    shifts = [(1, 1), (1, 3), (2, 0), (0, 1), (0, 3), (1, 0), (3, 0)] if nx == 4 else [(0, 1)]
    near = [lax.rem(y + ny - b, ny) * nx + lax.rem(x + nx - a, nx) for a, b in shifts]
    near_from = [lax.rem(y + b, ny) * nx + lax.rem(x + a, nx) for a, b in shifts]

    def send_near(phase, src, dst):
        for other in near:
            send(phase, src, dst, other, s)

    def forward(which):
        send(8, gp.at[core, which], gp.at[core, which], d, s + 1 - 2 * core)

    def grad_piece(which):
        row = pl.multiple_of(which // groups * 16, 16)
        column = pl.multiple_of(which % groups * 128, 128)
        return grad_v.at[pl.ds(row, 16), pl.ds(column, 128)]

    load_grad.wait()
    rs_buf[d] = grad_piece(mine)[...]
    pl.semaphore_wait(barrier, ns + nd - 2)

    @pl.loop(0, nd - 1)
    def _(k):
        other = over_groups(k)
        send(0, grad_piece(part_of(other)), rs_buf.at[d], other, s)

    load_stat.wait()
    most = jnp.sum(jnp.abs(stat_v[...]), axis=1, keepdims=True)
    bound = jnp.max(most, axis=0, keepdims=True)
    inverse = 1.0 / (bound * SMALL)
    mh[0], ml[0] = halves((stat_v[...] * SMALL) * inverse)
    load_stale.wait()
    load_owners.wait()
    load_refresh.wait()

    def product(first, second, result, alpha, beta, both):
        if both:
            pair = jnp.concatenate([mh[first], ml[first]], 1)
            total = dot(pair, jnp.concatenate([mh[second], mh[second]], 0))
        else:
            total = dot(mh[first], mh[second])
        kept = mh[second].astype(F32) + ml[second].astype(F32)
        total = alpha * kept + beta * total
        if result == 7:
            mh[result] = total.astype(BF16)
        else:
            mh[result], ml[result] = halves(total)

    for base in (0, 3, 6):
        product(base, base, base + 1, -0.625, 0.0625, False)
        if base < 6:
            product(base + 1, base + 1, base + 2, 3.125, 1.0, False)
            product(base + 2, base, base + 3, 2.44140625, 1.0, True)

    column = lax.broadcasted_iota(jnp.int32, (64, width), 1)
    line = lax.broadcasted_iota(jnp.int32, (64, width), 0)
    picked = jnp.where(column == line + 64 * mine, 1.0, 0.0)

    def apply(slot, value, alpha, beta):
        total = dot(jnp.concatenate(halves(value), 0), mh[slot], NT)
        return alpha * value + beta * (total[:64] + total[64:])

    left = apply(3, apply(0, picked, 1.25, -0.25), 1.25, -0.25)
    first = apply(6, left, 0.0, 1.0)
    second = apply(6, first, 0.0, 1.0)
    left = 1.25 * left - 0.25 * first
    right = 1.25 * first - 0.25 * second
    right = apply(7, apply(7, right, 1.5625, 1.0), 1.5625, 1.0)
    fresh = (1.25 * left - 0.25 * right) * lax.rsqrt(jnp.sqrt(bound))
    stale = dot(picked.astype(BF16), stale_v[...], NT)
    flag = jnp.int32(0)
    for f in range(4):
        flag = flag + jnp.where(owners[f] == s, refresh[f // 2], 0)
    chosen = jnp.full((64, width), flag, jnp.int32) > 0
    root = jnp.where(chosen, fresh, stale)

    quarter = lax.broadcasted_iota(jnp.int32, (16, 128), 1) // 32
    half = quarter // 2
    for g in range(groups):
        tiles = [root[16 * q:16 * q + 16, 128 * g:128 * g + 128] for q in range(4)]
        tiles = swap(tiles, quarter, 4)
        for p in range(4):
            x_send[4 * g + p] = tiles[p].astype(BF16)
    x_buf[s] = x_send[t]

    whole(0, rs_buf.at[pl.ds(0, nd - 1)]).wait_recv()
    summed = rs_buf[0].astype(F32)
    for k in range(1, nd):
        summed = summed + rs_buf[k].astype(F32)
    here = pl.ds(pl.multiple_of(z * 16, 16), 16)
    gp[core, mine, here] = (summed * (1.0 / nd)).astype(BF16)

    @pl.loop(0, nz - 1)
    def _(k):
        spot = gp.at[core, mine, here]
        send(1, spot, spot, d, block * nh + (z + far(k, nz)) % nz * 2 + core)

    @pl.loop(0, ns - 1)
    def _(k):
        other = over_shards(k)
        send(3, x_send.at[lax.rem(other, nh)], x_buf.at[s], d, other)

    whole(1, gp.at[0, 0, pl.ds(0, span - 16)]).wait_recv()
    spot = gp.at[core, mine]
    for k, other in enumerate(near):
        send(9 + k, spot, spot, other, s)
    forward(mine)

    whole(3, x_buf.at[pl.ds(0, ns - 1)]).wait_recv()

    piece = x_buf[owners[2 * block + 1]]
    r_send[...] = piece
    r_buf[t] = piece

    @pl.loop(0, nh - 1)
    def _(k):
        send(4, r_send, r_buf.at[t], d, over_block(k))

    piece = x_buf[owners[2 * block]]
    l_send[...] = piece
    l_buf[mine] = piece
    send_near(5, l_send, l_buf.at[mine])

    whole(5, l_buf.at[pl.ds(0, pieces - 1)]).wait_recv()
    for k in range(pieces):
        tile = l_buf[k].astype(F32)
        for q in range(4):
            row = q * span + 16 * k
            turned = tile if q == 0 else pltpu.roll(tile, 128 - 32 * q, 1)
            lt_v[row:row + 16] = turned.astype(BF16)

    whole(4, r_buf.at[pl.ds(0, nh - 1)]).wait_recv()
    parts = []
    for g in range(groups):
        tiles = [r_buf[4 * g + p].astype(F32) for p in range(4)]
        parts.append(jnp.concatenate(swap(tiles, quarter, 4), 0))
    right_root = jnp.concatenate(parts, 1).astype(BF16)

    for k in reversed(range(pieces - 1)):
        whole(9 + k, gp.at[0, 0]).wait_recv()
        forward(part_of(near_from[k]))

    def tile_part(c):
        grad = jnp.concatenate([
            jnp.concatenate([gp[c, h * groups + g] for g in range(groups)], 1) for h in range(2)
        ], 0)
        rows = pl.ds(pl.multiple_of(c * 2 * span, 2 * span), 2 * span)
        return dot(dot(right_root, grad, NT).astype(BF16), lt_v[rows])

    turned = tile_part(core)
    whole(8, gp.at[0]).wait_recv()
    other = tile_part(1 - core)
    turned = turned + other
    turned = jnp.concatenate([turned, jnp.zeros((64, 128), F32)], 0).T
    tile = jnp.where(half == 0, turned[0:16], pltpu.roll(turned[16:32], 64, 1))
    t_buf[mine] = tile.astype(BF16)
    send_near(6, t_buf.at[mine], t_buf.at[mine])

    def grad_square(k, total):
        tile = gp[k // pieces, k % pieces].astype(F32)
        tile = tile * tile
        return total + jnp.sum(tile.reshape(span // 8, 8, 128), axis=0)

    grad_sq = lax.fori_loop(0, 2 * pieces, grad_square, jnp.zeros((8, 128), F32))
    grad_sum = jnp.sum(jnp.sum(grad_sq, axis=1, keepdims=True), axis=0, keepdims=True)

    whole(6, t_buf.at[pl.ds(0, pieces - 1)]).wait_recv()
    rows = [
        swap([t_buf[2 * g].astype(F32), t_buf[2 * g + 1].astype(F32)], half, 2)
        for g in range(groups)
    ]
    square = sum(tile * tile for part in rows for tile in part)
    n_buf[t] = square[:8] + square[8:]

    @pl.loop(0, nh - 1)
    def _(k):
        spot = n_buf.at[t]
        send(7, spot, spot, d, over_block(k))

    whole(7, n_buf.at[pl.ds(0, nh - 1)]).wait_recv()
    square = sum(n_buf[k] for k in range(nh))
    square = jnp.sum(jnp.sum(square, axis=1, keepdims=True), axis=0, keepdims=True)
    scale = jnp.sqrt(grad_sum) * lax.rsqrt(square + 1e-6)
    for g in range(groups):
        for u in range(2):
            out_ref[16 * u:16 * u + 16, 128 * g:128 * g + 128] = rows[g][u] * scale

    whole(0, rs_buf.at[pl.ds(0, nd - 1)]).wait_send()
    whole(1, gp.at[0, 0, pl.ds(0, span - 16)]).wait_send()
    for k in range(pieces - 1):
        whole(9 + k, gp.at[0, 0]).wait_send()
    whole(3, x_buf.at[pl.ds(0, ns - 1)]).wait_send()
    whole(4, r_buf.at[pl.ds(0, nh - 1)]).wait_send()
    whole(5, l_buf.at[pl.ds(0, pieces - 1)]).wait_send()
    whole(6, t_buf.at[pl.ds(0, pieces - 1)]).wait_send()
    whole(7, n_buf.at[pl.ds(0, nh - 1)]).wait_send()
    whole(8, gp.at[0]).wait_send()


def per_device(nd, ns, grad_parts, params, momentum, statistics, stale_roots, owners, refresh):
    width = params.shape[1]
    nh = ns // 2
    pieces = width // 64
    direction = pl.pallas_call(
        functools.partial(kernel, nd, ns),
        out_shape=jax.ShapeDtypeStruct(params.shape, F32),
        in_specs=[pl.BlockSpec(memory_space=pltpu.HBM)] * 5,
        out_specs=pl.BlockSpec(memory_space=pltpu.VMEM),
        scratch_shapes=[
            pltpu.SMEM(owners.shape, jnp.int32),
            pltpu.SMEM(refresh.shape, jnp.int32),
            pltpu.VMEM(params.shape, BF16),
            pltpu.VMEM((width, width), F32),
            pltpu.VMEM((width, width), BF16),
            pltpu.VMEM((8, width, width), BF16),
            pltpu.VMEM((8, width, width), BF16),
            pltpu.VMEM((nd, 16, 128), BF16),
            pltpu.VMEM((2, pieces, 8 * nh, 128), BF16),
            pltpu.VMEM((nh, 16, 128), BF16),
            pltpu.VMEM((ns, 16, 128), BF16),
            pltpu.VMEM((16, 128), BF16),
            pltpu.VMEM((16, 128), BF16),
            pltpu.VMEM((pieces, 16, 128), BF16),
            pltpu.VMEM((nh, 16, 128), BF16),
            pltpu.VMEM((width, 128), BF16),
            pltpu.VMEM((pieces, 16, 128), BF16),
            pltpu.VMEM((nh, 8, 128), F32),
            pltpu.SemaphoreType.DMA((5,)),
            pltpu.SemaphoreType.DMA((8 + pieces,)),
            pltpu.SemaphoreType.DMA((8 + pieces,)),
        ],
        compiler_params=pltpu.CompilerParams(
            collective_id=0, has_side_effects=True, vmem_limit_bytes=63 * 2 ** 20
        ),
    )(owners, refresh, grad_parts, statistics, stale_roots)
    new_momentum = 0.9 * momentum + direction
    return params - 0.1 * new_momentum, new_momentum


def solution(mesh):
    rows = P("shard", None)
    body = functools.partial(per_device, mesh.shape["dp"], mesh.shape["shard"])
    return jax.shard_map(
        body,
        mesh=mesh,
        in_specs=(P("dp", "shard", None), rows, rows, rows, rows, P(), P()),
        out_specs=(rows, rows),
        check_vma=False,
    )
```
